256 devices in a mesh: aux: 64 (over y, z, core), occ: 4 (over x).
Axes of the slice: x: 4, y: 4, z: 8, core: 2. Of those that a mesh axis runs over, the one named last changes fastest.
Arguments:
- integrals: bfloat16 [8192, 64, 512], P('aux'), may hold values from -6 to 6
- slot_row_block: int32 [8192], P('aux'), may hold values from 0 to 511
- slot_column_block: int32 [8192], P('aux'), may hold values from 0 to 511
- shard_live_slots: int32 [64], P('aux'), may hold values from 32 to 128, as said below
- orbitals: bfloat16 [128, 32768], P('occ'), may hold values from -0.06982422 to 0.06982422
Outputs:
- exchange_applied: float32 [128, 32768], P(None, ('aux', 'occ'))
The draws below stay inside these ranges and needn't reach their ends.
Inputs may be any that keep to these rules, and one draw needn't show every extreme that they name: `shard_live_slots`: some shard has all 128 slots live in every draw.
All inputs are finite; a program needn't handle non-finite values.
Results may differ from the reference program's by a relative error of at most 0.0033.
Values may be sent and summed in bfloat16 or wider, within the bound.
A program may use at most 256 MiB of HBM per device.

```python
import jax
import jax.numpy as jnp
from jax import lax

BLOCK_SIDE = 64
NB = 32768
OCC = 128
AUXILIARY_SHARD = 8
NBLK_DEV = 128
BASIS_BLOCKS = 512
SLOTS_TOTAL = 8192
N_AUX = 64


def draw_shard_live_slots(key, part):
    key = jax.random.fold_in(key, 11)
    first_key, second_key = jax.random.split(key)
    counts = jax.random.randint(first_key, (N_AUX,), max(1, NBLK_DEV // 4), NBLK_DEV + 1, dtype=jnp.int32)
    full_shard = jax.random.randint(second_key, (), 0, N_AUX, dtype=jnp.int32)
    positions = jnp.arange(N_AUX, dtype=jnp.int32)
    return jnp.where(positions == full_shard, jnp.int32(NBLK_DEV), counts).astype(jnp.int32)


def touch_ends(array, rng, low, high):
    index_at = [jax.random.randint(jax.random.fold_in(rng, axis), (), 0, length) for axis, length in enumerate(array.shape)]
    main_axis = array.shape.index(max(array.shape))
    beside = index_at[:main_axis] + [(index_at[main_axis] + 1) % array.shape[main_axis]] + index_at[main_axis + 1:]
    return array.at[tuple(index_at)].set(low).at[tuple(beside)].set(high)


def block_levels(rng, dims, cuts, low, top_value):
    loudness, own = 1.0, jax.random.fold_in(rng, 6)
    for position, parts in cuts:
        steps = jnp.exp(jax.random.uniform(jax.random.fold_in(own, position), (parts,), jnp.float32, low / len(cuts), top_value / len(cuts)))
        loudness = loudness * jnp.repeat(steps, dims[position] // parts).reshape([-1 if axis == position else 1 for axis in range(len(dims))])
    return loudness


def gaussian(rng, shape, spread, bound, cuts=(), kind=jnp.bfloat16):
    drawn = spread * jax.random.normal(rng, shape, jnp.float32)
    if cuts:
        drawn = drawn * block_levels(rng, shape, cuts, -0.22, 0.18)
    return jnp.clip(drawn, -bound, bound).astype(kind)


def setup_inputs(seed: int = 0) -> dict:
    arg_keys = jax.random.split(jax.random.key(seed), 6)
    return {
        "integrals": gaussian(arg_keys[0], (SLOTS_TOTAL, BLOCK_SIDE, AUXILIARY_SHARD * BLOCK_SIDE), 1.0, 6.0, ((0, 64),)),
        "slot_row_block": touch_ends(jax.random.randint(arg_keys[1], (SLOTS_TOTAL,), 0, BASIS_BLOCKS), jax.random.fold_in(arg_keys[1], 1), 0, BASIS_BLOCKS - 1).astype(jnp.int32),
        "slot_column_block": touch_ends(jax.random.randint(arg_keys[2], (SLOTS_TOTAL,), 0, BASIS_BLOCKS), jax.random.fold_in(arg_keys[2], 1), 0, BASIS_BLOCKS - 1).astype(jnp.int32),
        "shard_live_slots": draw_shard_live_slots(jax.random.fold_in(arg_keys[5], 71), 0),
        "orbitals": gaussian(arg_keys[4], (OCC, NB), 0.011, 0.06982422, ((0, 4),)),
    }


def shard_term(integral_set, row_index_list, col_ids, live_count, orbitals):
    block_total = NB // BLOCK_SIDE
    orb_blocks = orbitals.reshape(OCC, block_total, BLOCK_SIDE)
    picked = jnp.take(orb_blocks, col_ids, axis=1)
    contrib = jnp.einsum('jkl,klx->kjx', picked.astype(jnp.float32), integral_set.astype(jnp.float32))
    live_slot = jnp.arange(NBLK_DEV, dtype=jnp.int32) < live_count
    contrib = jnp.where(live_slot[:, None, None], contrib, jnp.float32(0.0))
    half_done = jnp.zeros((block_total, OCC, AUXILIARY_SHARD * BLOCK_SIDE), jnp.float32).at[row_index_list].add(contrib)
    half_done = half_done.astype(jnp.bfloat16)
    split_half = half_done.reshape(block_total, OCC, AUXILIARY_SHARD, BLOCK_SIDE).astype(jnp.float32)
    fitted = jnp.einsum('rjpx,irx->pji', split_half, orb_blocks.astype(jnp.float32)).astype(jnp.bfloat16)
    applied = jnp.einsum('pji,rjpx->irx', fitted.astype(jnp.float32), split_half)
    return applied.reshape(OCC, NB)


def reference(integrals, slot_row_block, slot_column_block, shard_live_slots, orbitals):
    integral_sets = integrals.reshape(N_AUX, NBLK_DEV, BLOCK_SIDE, AUXILIARY_SHARD * BLOCK_SIDE)
    row_sets = slot_row_block.reshape(N_AUX, NBLK_DEV)
    col_sets = slot_column_block.reshape(N_AUX, NBLK_DEV)

    def accumulate(summed, inputs):
        integral_set, row_index_list, col_ids, live_count = inputs
        return summed + shard_term(integral_set, row_index_list, col_ids, live_count, orbitals), None

    summed, unused = lax.scan(accumulate, jnp.zeros((OCC, NB), jnp.float32), (integral_sets, row_sets, col_sets, shard_live_slots))
    return summed
```

```python
import functools

import jax
import jax.numpy as jnp
from jax import lax
from jax.experimental import pallas as pl
from jax.experimental.pallas import tpu as pltpu
from jax.sharding import PartitionSpec as P

MESH = pl.DeviceIdType.MESH
SLOTS = 128
SIDE = 64
NAUX = 8
NCHUNK = 8
CSLOTS = SLOTS // NCHUNK
CL = CSLOTS * SIDE
F32 = jnp.float32
BF16 = jnp.bfloat16


def swap_halves(v):
    return pltpu.roll(v, SIDE, v.ndim - 1)


def low_lanes(shape):
    return lax.broadcasted_iota(jnp.int32, shape, len(shape) - 1) < SIDE


def gather_pair(table, i0, i1):
    a, b = table[i0], table[i1]
    return jnp.where(low_lanes(a.shape), a, b)


def exchange_kernel(cols, rows, integrals, orbitals, out,
                    orb, table, ints, gath, rbuf, hbuf, facc,
                    orb_sem, int_sem, send_l, send_r, send_f, recv_l, recv_r, recv_f):
    aux, me = lax.axis_index("aux"), lax.axis_index("occ")
    right, left = lax.rem(me + 1, 4), lax.rem(me + 3, 4)
    orb_copy = pltpu.make_async_copy(orbitals, orb, orb_sem)
    orb_copy.start()

    def int_copy(c):
        return pltpu.make_async_copy(
            integrals.at[pl.ds(c * CSLOTS, CSLOTS)], ints.at[pl.ds(c * CSLOTS, CSLOTS)], int_sem.at[c])

    for c in range(NCHUNK):
        int_copy(c).start()

    barrier = pltpu.get_barrier_semaphore()
    for other in (left, right):
        pl.semaphore_signal(barrier, inc=1, device_id=(aux, other), device_id_type=MESH)
    pl.semaphore_wait(barrier, 2)
    orb_copy.wait()

    table[512] = jnp.zeros((32, 128), BF16)

    @pl.loop(0, 256, unroll=4)
    def _(k):
        t = orb[:, pl.ds(pl.multiple_of(k * 128, 128), 128)]
        table[k] = t
        table[256 + k] = swap_halves(t.astype(F32)).astype(BF16)

    def part(c, owner):
        return gath.at[c, pl.ds(pl.multiple_of(owner * 32, 32), 32)]

    def send(c, owner, to, ssem, rsem):
        return pltpu.make_async_remote_copy(
            src_ref=part(c, owner), dst_ref=part(c, owner), send_sem=ssem.at[c], recv_sem=rsem.at[c],
            device_id=(aux, to), device_id_type=MESH)

    def to_left(c):
        return send(c, me, left, send_l, recv_r)

    def to_right(c):
        return send(c, me, right, send_r, recv_l)

    def onward(c):
        if c % 2 == 0:
            return send(c, left, right, send_f, recv_f)
        return send(c, right, left, send_f, recv_f)

    for c in range(NCHUNK):
        @pl.loop(0, CSLOTS // 2, unroll=True)
        def _(k, c=c):
            s0 = c * CSLOTS + 2 * k
            lanes = pl.ds(pl.multiple_of(k * 128, 128), 128)
            gath[c, pl.ds(pl.multiple_of(me * 32, 32), 32), lanes] = gather_pair(table, cols[s0], cols[s0 + 1])
        to_left(c).start()
        to_right(c).start()

    for c in range(NCHUNK):
        @pl.loop(0, CSLOTS // 2, unroll=True)
        def _(k, c=c):
            s0 = c * CSLOTS + 2 * k
            lanes = pl.ds(pl.multiple_of(k * 128, 128), 128)
            rbuf[c, :, lanes] = gather_pair(table, rows[s0], rows[s0 + 1])

    facc[...] = jnp.zeros_like(facc)

    def compute(c):
        int_copy(c).wait()

        @pl.loop(0, CSLOTS // 2)
        def _(k):
            lanes = pl.ds(pl.multiple_of(k * 128, 128), 128)
            lhs = gath[c, :, lanes]
            s0 = c * CSLOTS + 2 * k
            low = low_lanes((SIDE, 128))
            for t in range(NAUX // 2):
                a = ints[s0, :, t * 128:(t + 1) * 128].astype(F32)
                b = ints[s0 + 1, :, t * 128:(t + 1) * 128].astype(F32)
                sa, sb = swap_halves(a), swap_halves(b)
                even = jnp.concatenate([jnp.where(low, a, 0.0), jnp.where(low, 0.0, sb)], 0)
                odd = jnp.concatenate([jnp.where(low, sa, 0.0), jnp.where(low, 0.0, b)], 0)
                w = jnp.concatenate([even, odd], 1).astype(BF16)
                h = jnp.dot(lhs, w, preferred_element_type=F32).astype(BF16)
                hbuf[c, 2 * t * 128:(2 * t + 1) * 128, lanes] = h[:, :128]
                hbuf[c, (2 * t + 1) * 128:(2 * t + 2) * 128, lanes] = h[:, 128:]

        @pl.loop(0, NAUX)
        def _(p):
            here = pl.ds(pl.multiple_of(p * 128, 128), 128)
            facc[here, :] += lax.dot_general(
                hbuf[c, here, :], rbuf[c], (((1,), (1,)), ((), ())), preferred_element_type=F32)

    for c in range(NCHUNK):
        to_left(c).wait_recv()
        to_right(c).wait_recv()
        onward(c).start()
        if c > 0:
            onward(c - 1).wait_recv()
            compute(c - 1)
    onward(NCHUNK - 1).wait_recv()
    compute(NCHUNK - 1)

    fit = jnp.transpose(facc[...]).astype(BF16)
    for c in range(NCHUNK):
        out[:, c * CL:(c + 1) * CL] = jnp.dot(fit, hbuf[c], preferred_element_type=F32)
    for c in range(NCHUNK):
        to_left(c).wait_send()
        to_right(c).wait_send()
        onward(c).wait_send()


def applied_slots(cols, rows, integrals, orbitals):
    sem = pltpu.SemaphoreType.DMA
    return pl.pallas_call(
        exchange_kernel,
        out_shape=jax.ShapeDtypeStruct((32, SLOTS * SIDE), F32),
        in_specs=[pl.BlockSpec(memory_space=pltpu.SMEM)] * 2 + [pl.BlockSpec(memory_space=pl.ANY)] * 2,
        out_specs=pl.BlockSpec(memory_space=pltpu.VMEM),
        scratch_shapes=[
            pltpu.VMEM((32, 32768), BF16),
            pltpu.VMEM((513, 32, 128), BF16),
            pltpu.VMEM((SLOTS, SIDE, NAUX * SIDE), BF16),
            pltpu.VMEM((NCHUNK, 128, CL), BF16),
            pltpu.VMEM((NCHUNK, 32, CL), BF16),
            pltpu.VMEM((NCHUNK, NAUX * 128, CL), BF16),
            pltpu.VMEM((NAUX * 128, 32), F32),
            sem, sem((NCHUNK,)),
            sem((NCHUNK,)), sem((NCHUNK,)), sem((NCHUNK,)),
            sem((NCHUNK,)), sem((NCHUNK,)), sem((NCHUNK,)),
        ],
        compiler_params=pltpu.CompilerParams(
            collective_id=0, has_side_effects=True, vmem_limit_bytes=56 * 1024 * 1024),
    )(cols, rows, integrals, orbitals)


def reduce_kernel(inv, prev, terms, out,
                  e2, own, cbuf, crecv, ya, yb, ydl, ydr, ym_l, ym_r, yrl, yrr, yta, ytb, zsend, zrecv, xsend,
                  csend_sem, crecv_sem, ysend_sem, yrecv_sem, zsend_sem, zrecv_sem, xsend_sem, xrecv_sem):
    aux, me = lax.axis_index("aux"), lax.axis_index("occ")
    core = lax.rem(aux, 2)
    z = lax.rem(aux // 2, 8)
    y = aux // 16

    def at(yy, zz, cc):
        return ((yy * 8 + zz) * 2 + cc, me)

    other_core = at(y, z, 1 - core)
    up, down, far = lax.rem(y + 1, 4), lax.rem(y + 3, 4), lax.rem(y + 2, 4)
    dev_up, dev_down = at(up, z, core), at(down, z, core)

    barrier = pltpu.get_barrier_semaphore()
    peers = [other_core, dev_up, dev_down]
    peers += [at(y, lax.rem(z + d, 8), core) for d in range(1, 8)]
    peers += [(aux, lax.rem(me + d, 4)) for d in range(1, 4)]
    for peer in peers:
        pl.semaphore_signal(barrier, inc=1, device_id=peer, device_id_type=MESH)

    e2[SLOTS] = jnp.zeros((32, 128), F32)

    @pl.loop(0, SLOTS // 2)
    def _(k):
        t = terms[:, pl.ds(pl.multiple_of(k * 128, 128), 128)]
        s = swap_halves(t)
        low = low_lanes(t.shape)
        e2[2 * k] = jnp.where(low, t, s) + e2[prev[2 * k]]
        e2[2 * k + 1] = jnp.where(low, s, t) + e2[prev[2 * k + 1]]

    def dense(q):
        a, b = e2[inv[2 * q]], e2[inv[2 * q + 1]]
        return jnp.where(low_lanes(a.shape), a, b)

    pl.semaphore_wait(barrier, 13)

    order = [far, up, down, y]

    def core_copy(n):
        return pltpu.make_async_remote_copy(
            src_ref=cbuf.at[n], dst_ref=crecv.at[n], send_sem=csend_sem.at[n], recv_sem=crecv_sem.at[n],
            device_id=other_core, device_id_type=MESH)

    for n in range(4):
        @pl.loop(0, 32)
        def _(m, n=n):
            q = order[n] * 64 + (m // 4) * 8 + (1 - core) * 4 + m % 4
            cbuf[n, m] = dense(q).astype(BF16)
        core_copy(n).start()

    for n in range(4):
        @pl.loop(0, 32)
        def _(m, n=n):
            q = order[n] * 64 + (m // 4) * 8 + core * 4 + m % 4
            own[n, m] = dense(q)

    def summed(n, m):
        return own[n, m] + crecv[n, m].astype(F32)

    def y_copy(k, src, dst, dev):
        return pltpu.make_async_remote_copy(
            src_ref=src, dst_ref=dst, send_sem=ysend_sem.at[k], recv_sem=yrecv_sem.at[k],
            device_id=dev, device_id_type=MESH)

    t_up = y_copy(0, ya, yta, dev_up)
    t_down = y_copy(1, yb, ytb, dev_down)
    d_up = y_copy(2, ydl, yrl.at[pl.ds(16, 16)], dev_up)
    d_down = y_copy(3, ydr, yrr.at[pl.ds(0, 16)], dev_down)
    m_up = y_copy(4, ym_l, yrl.at[pl.ds(0, 16)], dev_up)
    m_down = y_copy(5, ym_r, yrr.at[pl.ds(16, 16)], dev_down)

    core_copy(0).wait_recv()

    @pl.loop(0, 16)
    def _(m):
        ya[m] = summed(0, m).astype(BF16)
        yb[m] = summed(0, m + 16).astype(BF16)
    t_up.start()
    t_down.start()
    core_copy(1).wait_recv()

    @pl.loop(0, 16)
    def _(m):
        ydl[m] = summed(1, m + 16).astype(BF16)
    d_up.start()
    core_copy(2).wait_recv()

    @pl.loop(0, 16)
    def _(m):
        ydr[m] = summed(2, m).astype(BF16)
    d_down.start()
    t_up.wait_recv()

    @pl.loop(0, 16)
    def _(m):
        ym_l[m] = (summed(1, m) + yta[m].astype(F32)).astype(BF16)
    m_up.start()
    t_down.wait_recv()

    @pl.loop(0, 16)
    def _(m):
        ym_r[m] = (summed(2, m + 16) + ytb[m].astype(F32)).astype(BF16)
    m_down.start()
    core_copy(3).wait_recv()
    d_up.wait_recv()
    d_down.wait_recv()
    m_up.wait_recv()
    m_down.wait_recv()

    @pl.loop(0, 32)
    def _(m):
        v = summed(3, m) + yrl[m].astype(F32) + yrr[m].astype(F32)
        own[3, m] = v
        zsend[m] = v.astype(BF16)

    def z_copy(d):
        to = lax.rem(z + d, 8)
        return pltpu.make_async_remote_copy(
            src_ref=zsend.at[pl.ds(pl.multiple_of(to * 4, 4), 4)], dst_ref=zrecv.at[d - 1],
            send_sem=zsend_sem.at[d - 1], recv_sem=zrecv_sem.at[d - 1],
            device_id=at(y, to, core), device_id_type=MESH)

    for d in (4, 3, 5, 2, 6, 1, 7):
        z_copy(d).start()
    for d in range(1, 8):
        z_copy(d).wait_recv()

    @pl.loop(0, 4)
    def _(m):
        v = own[3, z * 4 + m]
        for d in range(7):
            v = v + zrecv[d, m].astype(F32)
        xsend[m] = v

    here = pl.ds(pl.multiple_of(me * 32, 32), 32)
    out[here, :] = xsend[me]

    def x_copy(d):
        to = lax.rem(me + d, 4)
        return pltpu.make_async_remote_copy(
            src_ref=xsend.at[to], dst_ref=out.at[here],
            send_sem=xsend_sem.at[d - 1], recv_sem=xrecv_sem.at[d - 1],
            device_id=(aux, to), device_id_type=MESH)

    for d in (2, 1, 3):
        x_copy(d).start()
    for n in range(4):
        core_copy(n).wait_send()
    for cp in (t_up, t_down, d_up, d_down, m_up, m_down):
        cp.wait_send()
    for d in range(1, 8):
        z_copy(d).wait_send()
    for d in range(1, 4):
        x_copy(d).wait()


def reduced(inv, prev, terms):
    sem = pltpu.SemaphoreType.DMA
    half = (16, 32, 128)
    return pl.pallas_call(
        reduce_kernel,
        out_shape=jax.ShapeDtypeStruct((128, 128), F32),
        in_specs=[pl.BlockSpec(memory_space=pltpu.SMEM)] * 2 + [pl.BlockSpec(memory_space=pltpu.VMEM)],
        out_specs=pl.BlockSpec(memory_space=pltpu.VMEM),
        scratch_shapes=[
            pltpu.VMEM((SLOTS + 1, 32, 128), F32),
            pltpu.VMEM((4, 32, 32, 128), F32),
            pltpu.VMEM((4, 32, 32, 128), BF16),
            pltpu.VMEM((4, 32, 32, 128), BF16),
            pltpu.VMEM(half, BF16), pltpu.VMEM(half, BF16), pltpu.VMEM(half, BF16), pltpu.VMEM(half, BF16),
            pltpu.VMEM(half, BF16), pltpu.VMEM(half, BF16),
            pltpu.VMEM((32, 32, 128), BF16), pltpu.VMEM((32, 32, 128), BF16),
            pltpu.VMEM(half, BF16), pltpu.VMEM(half, BF16),
            pltpu.VMEM((32, 32, 128), BF16),
            pltpu.VMEM((7, 4, 32, 128), BF16),
            pltpu.VMEM((4, 32, 128), F32),
            sem((4,)), sem((4,)), sem((6,)), sem((6,)), sem((7,)), sem((7,)), sem((3,)), sem((3,)),
        ],
        compiler_params=pltpu.CompilerParams(
            collective_id=1, has_side_effects=True, vmem_limit_bytes=48 * 1024 * 1024),
    )(inv, prev, terms)


def tile_of(block, slot):
    return ((block ^ slot) & 1) * 256 + (block >> 1)


def shards(integrals, slot_row_block, slot_column_block, shard_live_slots, orbitals):
    slot = jnp.arange(SLOTS, dtype=jnp.int32)
    rows = slot_row_block
    hit = rows[None, :] == jnp.arange(512, dtype=jnp.int32)[:, None]
    inv = jnp.max(jnp.where(hit, slot[None, :], -1), axis=1)
    inv = jnp.where(inv < 0, SLOTS, inv)
    same = (rows[None, :] == rows[:, None]) & (slot[None, :] < slot[:, None])
    prev = jnp.max(jnp.where(same, slot[None, :], -1), axis=1)
    prev = jnp.where(prev < 0, SLOTS, prev)
    col_at = jnp.where(slot < shard_live_slots[0], tile_of(slot_column_block, slot), 512)
    terms = applied_slots(col_at, tile_of(rows, slot), integrals, orbitals)
    return reduced(inv, prev, terms)


def solution(mesh):
    placed = (P("aux", None, None), P("aux"), P("aux"), P("aux"), P("occ", None))
    return jax.shard_map(
        shards, mesh=mesh, in_specs=placed, out_specs=P(None, ("aux", "occ")), check_vma=False
    )
```

```python
import jax
import jax.numpy as jnp
from jax import lax
from jax.experimental import pallas as pl
from jax.experimental.pallas import tpu as pltpu
from jax.sharding import PartitionSpec as P

MESH = pl.DeviceIdType.MESH
SLOTS = 128
SIDE = 64
NCHUNK = 8
CSLOTS = SLOTS // NCHUNK
CL = CSLOTS * SIDE
CT = CSLOTS * 128
TILES = 4
F32 = jnp.float32
BF16 = jnp.bfloat16


def swap_halves(v):
    return pltpu.roll(v, SIDE, v.ndim - 1)


def low_lanes(shape):
    return lax.broadcasted_iota(jnp.int32, shape, len(shape) - 1) < SIDE


def lanes_at(k, size):
    return pl.ds(pl.multiple_of(k * size, size), size)


def kernel(col_tile, col_pick, row_tile, row_pick, row_swap, inv, prev, integrals, orbitals, out,
           orb, table, cand, ints, gath, rr, hbuf, facc,
           e2, own, cbuf, crecv, ysend, yfar, yleft, yright, zsend, zrecv, xsend,
           orb_sem, int_sem, send_l, send_r, send_f, recv_l, recv_r, recv_f,
           csend_sem, crecv_sem, ysend_sem, yrecv_sem, zsend_sem, zrecv_sem, xsend_sem, xrecv_sem):
    aux, me = lax.axis_index("aux"), lax.axis_index("occ")
    right, left = lax.rem(me + 1, 4), lax.rem(me + 3, 4)
    core = lax.rem(aux, 2)
    z = lax.rem(aux // 2, 8)
    y = aux // 16

    def at(yy, zz, cc):
        return ((yy * 8 + zz) * 2 + cc, me)

    other_core = at(y, z, 1 - core)
    up, down, far = lax.rem(y + 1, 4), lax.rem(y + 3, 4), lax.rem(y + 2, 4)
    dev_up, dev_down = at(up, z, core), at(down, z, core)

    orb_copy = pltpu.make_async_copy(orbitals, orb, orb_sem)
    orb_copy.start()

    def int_copy(c):
        here = pl.ds(c * CL, CL)
        return pltpu.make_async_copy(integrals.at[here], ints.at[here], int_sem.at[c])

    barrier = pltpu.get_barrier_semaphore()
    peers = [other_core, dev_up, dev_down]
    peers += [at(y, lax.rem(z + d, 8), core) for d in range(1, 8)]
    peers += [(aux, lax.rem(me + d, 4)) for d in range(1, 4)]
    for peer in peers:
        pl.semaphore_signal(barrier, inc=1, device_id=peer, device_id_type=MESH)

    orb_copy.wait()
    for c in range(NCHUNK):
        int_copy(c).start()

    @pl.loop(0, 256, unroll=16)
    def _(k):
        table[k] = orb[:, lanes_at(k, 128)]
    cand[2 * SLOTS] = jnp.zeros((32, 128), BF16)

    def group(c, g):
        return gath.at[c, pl.ds(g * 32, 32)]

    def send(c, g_from, g_to, to, ssem, rsem):
        return pltpu.make_async_remote_copy(
            src_ref=group(c, g_from), dst_ref=group(c, g_to), send_sem=ssem.at[c], recv_sem=rsem.at[c],
            device_id=(aux, to), device_id_type=MESH)

    def to_left(c):
        return send(c, 0, 2, left, send_l, recv_r)

    def to_right(c):
        return send(c, 0, 1, right, send_r, recv_l)

    def onward(c):
        if c % 2 == 0:
            return send(c, 1, 3, right, send_f, recv_f)
        return send(c, 2, 3, left, send_f, recv_f)

    def candidates(tile, c):
        @pl.loop(0, CSLOTS, unroll=8)
        def _(k):
            s = c * CSLOTS + k
            t = table[tile[s]]
            cand[2 * s] = t
            cand[2 * s + 1] = swap_halves(t)

    for c in range(NCHUNK):
        candidates(col_tile, c)

        @pl.loop(0, CSLOTS // 2, unroll=4)
        def _(k, c=c):
            s = c * CSLOTS + 2 * k
            a, b = cand[col_pick[s]], cand[col_pick[s + 1]]
            gath[c, 0:32, lanes_at(k, 128)] = jnp.where(low_lanes(a.shape), a, b)
        if c == 0:
            pl.semaphore_wait(barrier, 13)
        to_left(c).start()
        to_right(c).start()

    for c in range(NCHUNK):
        candidates(row_tile, c)

        @pl.loop(0, CSLOTS, unroll=4)
        def _(k, c=c):
            s = c * CSLOTS + k
            a, b = cand[row_pick[s]], cand[row_swap[s]]
            low = low_lanes(a.shape)
            zero = jnp.zeros_like(a)
            rr[c, 0:32, lanes_at(k, 128)] = jnp.where(low, a, zero)
            rr[c, 32:64, lanes_at(k, 128)] = jnp.where(low, zero, b)

    facc[...] = jnp.zeros_like(facc)

    def half(c, first, count):
        @pl.loop(0, CSLOTS // 2, unroll=2)
        def _(k):
            g = gath[c, first:first + count, lanes_at(k, 128)]
            low = low_lanes(g.shape)
            zero = jnp.zeros_like(g)
            lhs = jnp.concatenate([jnp.where(low, g, zero), jnp.where(low, zero, g)], 0)
            w = ints[lanes_at(c * (CSLOTS // 2) + k, 128), :]
            h = jnp.dot(lhs, w, preferred_element_type=F32).astype(BF16)
            for t in range(TILES):
                for n in range(2):
                    hbuf[c, t * 128 + first:t * 128 + first + count, lanes_at(2 * k + n, 128)] = (
                        h[n * count:(n + 1) * count, t * 128:(t + 1) * 128])

    for c in range(NCHUNK):
        to_left(c).wait_recv()
        to_right(c).wait_recv()
        onward(c).start()
        int_copy(c).wait()
        half(c, 0, 96)
    for c in range(NCHUNK):
        onward(c).wait_recv()
        half(c, 96, 32)
        facc[...] += lax.dot_general(rr[c], hbuf[c], (((1,), (1,)), ((), ())), preferred_element_type=F32)

    fit = facc[...].astype(BF16)
    e2[SLOTS] = jnp.zeros((32, 128), F32)
    for c in range(NCHUNK):
        @pl.loop(0, CSLOTS // 4)
        def _(k, c=c):
            v = jnp.dot(fit, hbuf[c, :, lanes_at(k, 512)], preferred_element_type=F32)
            low = low_lanes((32, 128))
            for n in range(4):
                s = c * CSLOTS + 4 * k + n
                here = slice(n * 128, (n + 1) * 128)
                u = jnp.where(low, v[:32, here], v[32:, here])
                e2[s] = u + swap_halves(u)

    @pl.loop(0, SLOTS, unroll=8)
    def _(s):
        e2[s] = e2[s] + e2[prev[s]]

    order = [far, up, down, y]

    def dense(n, h, m, cc):
        q = order[n] * 64 + (m // 2) * 8 + cc * 4 + 2 * h + m % 2
        a, b = e2[inv[2 * q]], e2[inv[2 * q + 1]]
        return jnp.where(low_lanes(a.shape), a, b)

    def core_copy(n, h):
        k = h * 4 + n
        return pltpu.make_async_remote_copy(
            src_ref=cbuf.at[k], dst_ref=crecv.at[k], send_sem=csend_sem.at[k], recv_sem=crecv_sem.at[k],
            device_id=other_core, device_id_type=MESH)

    for h in range(2):
        for n in range(4):
            @pl.loop(0, 16, unroll=4)
            def _(m, n=n, h=h):
                cbuf[h * 4 + n, m] = dense(n, h, m, 1 - core).astype(BF16)
            core_copy(n, h).start()
    for h in range(2):
        for n in range(4):
            @pl.loop(0, 16, unroll=4)
            def _(m, n=n, h=h):
                own[h * 4 + n, m] = dense(n, h, m, core)

    def summed(n, h, m):
        return own[h * 4 + n, m] + crecv[h * 4 + n, m].astype(F32)

    def y_copy(h, k, dst, dev):
        return pltpu.make_async_remote_copy(
            src_ref=ysend.at[h, k], dst_ref=dst, send_sem=ysend_sem.at[h, k], recv_sem=yrecv_sem.at[h, k],
            device_id=dev, device_id_type=MESH)

    first, last = pl.ds(0, 8), pl.ds(8, 8)

    def y_copies(h):
        return (
            y_copy(h, 0, yfar.at[h, 0], dev_up),
            y_copy(h, 1, yfar.at[h, 1], dev_down),
            y_copy(h, 2, yleft.at[h, last], dev_up),
            y_copy(h, 3, yright.at[h, first], dev_down),
            y_copy(h, 4, yleft.at[h, first], dev_up),
            y_copy(h, 5, yright.at[h, last], dev_down),
        )

    for h in range(2):
        cp = y_copies(h)
        core_copy(0, h).wait_recv()

        @pl.loop(0, 8, unroll=4)
        def _(m, h=h):
            ysend[h, 0, m] = summed(0, h, m).astype(BF16)
            ysend[h, 1, m] = summed(0, h, m + 8).astype(BF16)
        cp[0].start()
        cp[1].start()
        core_copy(1, h).wait_recv()
        core_copy(2, h).wait_recv()

        @pl.loop(0, 8, unroll=4)
        def _(m, h=h):
            ysend[h, 2, m] = summed(1, h, m + 8).astype(BF16)
            ysend[h, 3, m] = summed(2, h, m).astype(BF16)
        cp[2].start()
        cp[3].start()
    for h in range(2):
        cp = y_copies(h)
        cp[0].wait_recv()
        cp[1].wait_recv()

        @pl.loop(0, 8, unroll=4)
        def _(m, h=h):
            ysend[h, 4, m] = (summed(1, h, m) + yfar[h, 0, m].astype(F32)).astype(BF16)
            ysend[h, 5, m] = (summed(2, h, m + 8) + yfar[h, 1, m].astype(F32)).astype(BF16)
        cp[4].start()
        cp[5].start()

    def z_copy(h, d):
        to = lax.rem(z + d, 8)
        return pltpu.make_async_remote_copy(
            src_ref=zsend.at[h, pl.ds(pl.multiple_of(to * 2, 2), 2)], dst_ref=zrecv.at[h, d - 1],
            send_sem=zsend_sem.at[h, d - 1], recv_sem=zrecv_sem.at[h, d - 1],
            device_id=at(y, to, core), device_id_type=MESH)

    for h in range(2):
        core_copy(3, h).wait_recv()
        for cp in y_copies(h)[2:]:
            cp.wait_recv()

        @pl.loop(0, 16, unroll=4)
        def _(m, h=h):
            v = summed(3, h, m) + yleft[h, m].astype(F32) + yright[h, m].astype(F32)
            own[h * 4 + 3, m] = v
            zsend[h, m] = v.astype(BF16)
        for d in (4, 3, 5, 2, 6, 1, 7):
            z_copy(h, d).start()
    for h in range(2):
        for d in range(1, 8):
            z_copy(h, d).wait_recv()
        for m in range(2):
            v = own[h * 4 + 3, z * 2 + m]
            for d in range(7):
                v = v + zrecv[h, d, m].astype(F32)
            xsend[2 * h + m] = v

    here = lanes_at(me, 32)
    out[here, :] = xsend[me]

    def x_copy(d):
        to = lax.rem(me + d, 4)
        return pltpu.make_async_remote_copy(
            src_ref=xsend.at[to], dst_ref=out.at[here],
            send_sem=xsend_sem.at[d - 1], recv_sem=xrecv_sem.at[d - 1],
            device_id=(aux, to), device_id_type=MESH)

    for d in (2, 1, 3):
        x_copy(d).start()
    for c in range(NCHUNK):
        to_left(c).wait_send()
        to_right(c).wait_send()
        onward(c).wait_send()
    for h in range(2):
        for n in range(4):
            core_copy(n, h).wait_send()
        for cp in y_copies(h):
            cp.wait_send()
        for d in range(1, 8):
            z_copy(h, d).wait_send()
    for d in range(1, 4):
        x_copy(d).wait()


def applied(col_tile, col_pick, row_tile, row_pick, row_swap, inv, prev, integrals, orbitals):
    sem = pltpu.SemaphoreType.DMA
    vmem = pltpu.VMEM
    return pl.pallas_call(
        kernel,
        out_shape=jax.ShapeDtypeStruct((128, 128), F32),
        in_specs=[pl.BlockSpec(memory_space=pltpu.SMEM)] * 7 + [pl.BlockSpec(memory_space=pl.ANY)] * 2,
        out_specs=pl.BlockSpec(memory_space=pltpu.VMEM),
        scratch_shapes=[
            vmem((32, 32768), BF16),
            vmem((256, 32, 128), BF16),
            vmem((2 * SLOTS + 1, 32, 128), BF16),
            vmem((SLOTS * SIDE, 512), BF16),
            vmem((NCHUNK, 128, CL), BF16),
            vmem((NCHUNK, 64, CT), BF16),
            vmem((NCHUNK, 512, CT), BF16),
            vmem((64, 512), F32),
            vmem((SLOTS + 1, 32, 128), F32),
            vmem((8, 16, 32, 128), F32),
            vmem((8, 16, 32, 128), BF16),
            vmem((8, 16, 32, 128), BF16),
            vmem((2, 6, 8, 32, 128), BF16),
            vmem((2, 2, 8, 32, 128), BF16),
            vmem((2, 16, 32, 128), BF16),
            vmem((2, 16, 32, 128), BF16),
            vmem((2, 16, 32, 128), BF16),
            vmem((2, 7, 2, 32, 128), BF16),
            vmem((4, 32, 128), F32),
            sem, sem((NCHUNK,)),
            sem((NCHUNK,)), sem((NCHUNK,)), sem((NCHUNK,)),
            sem((NCHUNK,)), sem((NCHUNK,)), sem((NCHUNK,)),
            sem((8,)), sem((8,)), sem((2, 6)), sem((2, 6)), sem((2, 7)), sem((2, 7)), sem((3,)), sem((3,)),
        ],
        compiler_params=pltpu.CompilerParams(
            collective_id=0, has_side_effects=True, vmem_limit_bytes=58 * 1024 * 1024),
    )(col_tile, col_pick, row_tile, row_pick, row_swap, inv, prev, integrals, orbitals)


def shards(integrals, slot_row_block, slot_column_block, shard_live_slots, orbitals):
    slot = jnp.arange(SLOTS, dtype=jnp.int32)
    rows, cols = slot_row_block, slot_column_block
    hit = rows[None, :] == jnp.arange(512, dtype=jnp.int32)[:, None]
    inv = jnp.max(jnp.where(hit, slot[None, :], -1), axis=1)
    inv = jnp.where(inv < 0, SLOTS, inv)
    same = (rows[None, :] == rows[:, None]) & (slot[None, :] < slot[:, None])
    prev = jnp.max(jnp.where(same, slot[None, :], -1), axis=1)
    prev = jnp.where(prev < 0, SLOTS, prev)
    col_pick = jnp.where(slot < shard_live_slots[0], 2 * slot + ((cols ^ slot) & 1), 2 * SLOTS)
    row_pick = 2 * slot + (rows & 1)
    return applied(cols >> 1, col_pick, rows >> 1, row_pick, row_pick ^ 1, inv, prev,
                   integrals.reshape(SLOTS * SIDE, 512), orbitals)


def solution(mesh):
    placed = (P("aux", None, None), P("aux"), P("aux"), P("aux"), P("occ", None))
    return jax.shard_map(
        shards, mesh=mesh, in_specs=placed, out_specs=P(None, ("aux", "occ")), check_vma=False
    )
```

```python
import jax
import jax.numpy as jnp
from jax import lax
from jax.experimental import pallas as pl
from jax.experimental.pallas import tpu as pltpu
from jax.sharding import PartitionSpec as P

MESH = pl.DeviceIdType.MESH
SLOTS = 128
SIDE = 64
NCHUNK = 8
CSLOTS = SLOTS // NCHUNK
CL = CSLOTS * SIDE
CT = CSLOTS * 128
TILES = 4
F32 = jnp.float32
BF16 = jnp.bfloat16


def swap_halves(v):
    return pltpu.roll(v, SIDE, v.ndim - 1)


def low_lanes(shape):
    return lax.broadcasted_iota(jnp.int32, shape, len(shape) - 1) < SIDE


def lanes_at(k, size):
    return pl.ds(pl.multiple_of(k * size, size), size)


def kernel(cols, rows, live, row_lanes, integrals, orbitals, out,
           orb, table, lists, maps, ints, gath, rr, hbuf, facc,
           e2, own, cbuf, crecv, ysend, yfar, yleft, yright, zsend, zrecv, xsend,
           orb_sem, map_sem, int_sem, send_l, send_r, send_f, recv_l, recv_r, recv_f,
           csend_sem, crecv_sem, ysend_sem, yrecv_sem, zsend_sem, zrecv_sem, xsend_sem, xrecv_sem):
    aux, me = lax.axis_index("aux"), lax.axis_index("occ")
    right, left = lax.rem(me + 1, 4), lax.rem(me + 3, 4)
    core = lax.rem(aux, 2)
    z = lax.rem(aux // 2, 8)
    y = aux // 16

    def at(yy, zz, cc):
        return ((yy * 8 + zz) * 2 + cc, me)

    other_core = at(y, z, 1 - core)
    up, down, far = lax.rem(y + 1, 4), lax.rem(y + 3, 4), lax.rem(y + 2, 4)
    dev_up, dev_down = at(up, z, core), at(down, z, core)

    orb_copy = pltpu.make_async_copy(orbitals, orb, orb_sem)
    orb_copy.start()

    def int_copy(c):
        here = pl.ds(c * CL, CL)
        return pltpu.make_async_copy(integrals.at[here], ints.at[here], int_sem.at[c])

    barrier = pltpu.get_barrier_semaphore()
    peers = [other_core, dev_up, dev_down]
    peers += [at(y, lax.rem(z + d, 8), core) for d in range(1, 8)]
    peers += [(aux, lax.rem(me + d, 4)) for d in range(1, 4)]
    for peer in peers:
        pl.semaphore_signal(barrier, inc=1, device_id=peer, device_id_type=MESH)

    across = jnp.broadcast_to(row_lanes[...], (SLOTS, 128))
    along = jnp.transpose(across)
    slot = lax.broadcasted_iota(jnp.int32, (SLOTS, 128), 0)
    lane = lax.broadcasted_iota(jnp.int32, (SLOTS, 128), 1)

    def last_of(hit):
        v = jnp.max(jnp.where(hit, slot, -1), axis=0, keepdims=True)
        return jnp.where(v < 0, SLOTS, v)

    for r in range(4):
        lists[r:r + 1, :] = last_of(along == lane + r * 128)
    lists[4:5, :] = last_of((along == across) & (slot < lane))
    lists[5:8, :] = jnp.full((3, 128), SLOTS, jnp.int32)
    map_copy = pltpu.make_async_copy(lists, maps, map_sem)
    map_copy.start()

    orb_copy.wait()
    for c in range(NCHUNK):
        int_copy(c).start()

    table[256] = jnp.zeros((32, 128), BF16)

    @pl.loop(0, 256, unroll=32)
    def _(k):
        table[k] = orb[:, lanes_at(k, 128)]

    def group(c, g):
        return gath.at[c, pl.ds(g * 32, 32)]

    def send(c, g_from, g_to, to, ssem, rsem):
        return pltpu.make_async_remote_copy(
            src_ref=group(c, g_from), dst_ref=group(c, g_to), send_sem=ssem.at[c], recv_sem=rsem.at[c],
            device_id=(aux, to), device_id_type=MESH)

    def to_left(c):
        return send(c, 0, 2, left, send_l, recv_r)

    def to_right(c):
        return send(c, 0, 1, right, send_r, recv_l)

    def onward(c):
        if c % 2 == 0:
            return send(c, 1, 3, right, send_f, recv_f)
        return send(c, 2, 3, left, send_f, recv_f)

    count = live[0]

    def column(s, half):
        b = cols[s]
        alive = jnp.minimum(jnp.maximum(count - s, 0), 1)
        return pltpu.roll(table[256 + ((b >> 1) - 256) * alive], ((b ^ half) & 1) * SIDE, 1)

    for c in range(NCHUNK):
        for k in range(CSLOTS // 2):
            s = c * CSLOTS + 2 * k
            a, b = column(s, 0), column(s + 1, 1)
            gath[c, 0:32, k * 128:(k + 1) * 128] = jnp.where(low_lanes(a.shape), a, b)
        if c == 0:
            pl.semaphore_wait(barrier, 13)
        to_left(c).start()
        to_right(c).start()

    for c in range(NCHUNK):
        @pl.loop(0, CSLOTS, unroll=CSLOTS)
        def _(k, c=c):
            b = rows[c * CSLOTS + k]
            t = table[b >> 1]
            a = pltpu.roll(t, (b & 1) * SIDE, 1)
            low = low_lanes(a.shape)
            zero = jnp.zeros_like(a)
            rr[c, 0:32, lanes_at(k, 128)] = jnp.where(low, a, zero)
            rr[c, 32:64, lanes_at(k, 128)] = jnp.where(low, zero, swap_halves(a))

    facc[...] = jnp.zeros_like(facc)

    def half(c, first, count):
        @pl.loop(0, CSLOTS // 2, unroll=8)
        def _(k):
            g = gath[c, first:first + count, lanes_at(k, 128)]
            low = low_lanes(g.shape)
            zero = jnp.zeros_like(g)
            lhs = jnp.concatenate([jnp.where(low, g, zero), jnp.where(low, zero, g)], 0)
            w = ints[lanes_at(c * (CSLOTS // 2) + k, 128), :]
            h = jnp.dot(lhs, w, preferred_element_type=F32).astype(BF16)
            for t in range(TILES):
                for n in range(2):
                    hbuf[c, t * 128 + first:t * 128 + first + count, lanes_at(2 * k + n, 128)] = (
                        h[n * count:(n + 1) * count, t * 128:(t + 1) * 128])

    for c in range(NCHUNK):
        to_left(c).wait_recv()
        to_right(c).wait_recv()
        onward(c).start()
        int_copy(c).wait()
        half(c, 0, 96)
    for c in range(NCHUNK):
        onward(c).wait_recv()
        half(c, 96, 32)
        facc[...] += lax.dot_general(rr[c], hbuf[c], (((1,), (1,)), ((), ())), preferred_element_type=F32)

    fit = facc[...].astype(BF16)
    map_copy.wait()
    e2[SLOTS] = jnp.zeros((32, 128), F32)
    for c in range(NCHUNK):
        @pl.loop(0, CSLOTS // 4, unroll=4)
        def _(k, c=c):
            v = jnp.dot(fit, hbuf[c, :, lanes_at(k, 512)], preferred_element_type=F32)
            low = low_lanes((32, 128))
            for n in range(4):
                s = c * CSLOTS + 4 * k + n
                here = slice(n * 128, (n + 1) * 128)
                u = jnp.where(low, v[:32, here], v[32:, here])
                e2[s] = u + swap_halves(u) + e2[maps[4, s]]

    order = [far, up, down, y]

    def dense(n, h, m, cc):
        row, col = order[n], 2 * ((m // 2) * 8 + cc * 4 + 2 * h + m % 2)
        a, b = e2[maps[row, col]], e2[maps[row, col + 1]]
        return jnp.where(low_lanes(a.shape), a, b)

    def core_copy(n, h):
        k = h * 4 + n
        return pltpu.make_async_remote_copy(
            src_ref=cbuf.at[k], dst_ref=crecv.at[k], send_sem=csend_sem.at[k], recv_sem=crecv_sem.at[k],
            device_id=other_core, device_id_type=MESH)

    for h in range(2):
        for n in range(4):
            @pl.loop(0, 16, unroll=16)
            def _(m, n=n, h=h):
                cbuf[h * 4 + n, m] = dense(n, h, m, 1 - core).astype(BF16)
            core_copy(n, h).start()
    for h in range(2):
        for n in range(4):
            @pl.loop(0, 16, unroll=16)
            def _(m, n=n, h=h):
                own[h * 4 + n, m] = dense(n, h, m, core)

    def summed(n, h, m):
        return own[h * 4 + n, m] + crecv[h * 4 + n, m].astype(F32)

    def y_copy(h, k, dst, dev):
        return pltpu.make_async_remote_copy(
            src_ref=ysend.at[h, k], dst_ref=dst, send_sem=ysend_sem.at[h, k], recv_sem=yrecv_sem.at[h, k],
            device_id=dev, device_id_type=MESH)

    first, last = pl.ds(0, 8), pl.ds(8, 8)

    def y_copies(h):
        return (
            y_copy(h, 0, yfar.at[h, 0], dev_up),
            y_copy(h, 1, yfar.at[h, 1], dev_down),
            y_copy(h, 2, yleft.at[h, last], dev_up),
            y_copy(h, 3, yright.at[h, first], dev_down),
            y_copy(h, 4, yleft.at[h, first], dev_up),
            y_copy(h, 5, yright.at[h, last], dev_down),
        )

    for h in range(2):
        cp = y_copies(h)
        core_copy(0, h).wait_recv()

        @pl.loop(0, 8, unroll=8)
        def _(m, h=h):
            ysend[h, 0, m] = summed(0, h, m).astype(BF16)
            ysend[h, 1, m] = summed(0, h, m + 8).astype(BF16)
        cp[0].start()
        cp[1].start()
        core_copy(1, h).wait_recv()
        core_copy(2, h).wait_recv()

        @pl.loop(0, 8, unroll=8)
        def _(m, h=h):
            ysend[h, 2, m] = summed(1, h, m + 8).astype(BF16)
            ysend[h, 3, m] = summed(2, h, m).astype(BF16)
        cp[2].start()
        cp[3].start()
    for h in range(2):
        cp = y_copies(h)
        cp[0].wait_recv()
        cp[1].wait_recv()

        @pl.loop(0, 8, unroll=8)
        def _(m, h=h):
            ysend[h, 4, m] = (summed(1, h, m) + yfar[h, 0, m].astype(F32)).astype(BF16)
            ysend[h, 5, m] = (summed(2, h, m + 8) + yfar[h, 1, m].astype(F32)).astype(BF16)
        cp[4].start()
        cp[5].start()

    def z_copy(h, d):
        to = lax.rem(z + d, 8)
        return pltpu.make_async_remote_copy(
            src_ref=zsend.at[h, pl.ds(pl.multiple_of(to * 2, 2), 2)], dst_ref=zrecv.at[h, d - 1],
            send_sem=zsend_sem.at[h, d - 1], recv_sem=zrecv_sem.at[h, d - 1],
            device_id=at(y, to, core), device_id_type=MESH)

    for h in range(2):
        core_copy(3, h).wait_recv()
        for cp in y_copies(h)[2:]:
            cp.wait_recv()

        @pl.loop(0, 16, unroll=16)
        def _(m, h=h):
            v = summed(3, h, m) + yleft[h, m].astype(F32) + yright[h, m].astype(F32)
            own[h * 4 + 3, m] = v
            zsend[h, m] = v.astype(BF16)
        for d in (4, 3, 5, 2, 6, 1, 7):
            z_copy(h, d).start()
    for h in range(2):
        for d in range(1, 8):
            z_copy(h, d).wait_recv()
        for m in range(2):
            v = own[h * 4 + 3, z * 2 + m]
            for d in range(7):
                v = v + zrecv[h, d, m].astype(F32)
            xsend[2 * h + m] = v

    here = lanes_at(me, 32)
    out[here, :] = xsend[me]

    def x_copy(d):
        to = lax.rem(me + d, 4)
        return pltpu.make_async_remote_copy(
            src_ref=xsend.at[to], dst_ref=out.at[here],
            send_sem=xsend_sem.at[d - 1], recv_sem=xrecv_sem.at[d - 1],
            device_id=(aux, to), device_id_type=MESH)

    for d in (2, 1, 3):
        x_copy(d).start()
    for c in range(NCHUNK):
        to_left(c).wait_send()
        to_right(c).wait_send()
        onward(c).wait_send()
    for h in range(2):
        for n in range(4):
            core_copy(n, h).wait_send()
        for cp in y_copies(h):
            cp.wait_send()
        for d in range(1, 8):
            z_copy(h, d).wait_send()
    for d in range(1, 4):
        x_copy(d).wait()


def applied(cols, rows, live, row_lanes, integrals, orbitals):
    sem = pltpu.SemaphoreType.DMA
    vmem = pltpu.VMEM
    return pl.pallas_call(
        kernel,
        out_shape=jax.ShapeDtypeStruct((128, 128), F32),
        in_specs=[pl.BlockSpec(memory_space=pltpu.SMEM)] * 3 + [pl.BlockSpec(memory_space=pltpu.VMEM)]
        + [pl.BlockSpec(memory_space=pl.ANY)] * 2,
        out_specs=pl.BlockSpec(memory_space=pltpu.VMEM),
        scratch_shapes=[
            vmem((32, 32768), BF16),
            vmem((257, 32, 128), BF16),
            vmem((8, 128), jnp.int32),
            pltpu.SMEM((8, 128), jnp.int32),
            vmem((SLOTS * SIDE, 512), BF16),
            vmem((NCHUNK, 128, CL), BF16),
            vmem((NCHUNK, 64, CT), BF16),
            vmem((NCHUNK, 512, CT), BF16),
            vmem((64, 512), F32),
            vmem((SLOTS + 1, 32, 128), F32),
            vmem((8, 16, 32, 128), F32),
            vmem((8, 16, 32, 128), BF16),
            vmem((8, 16, 32, 128), BF16),
            vmem((2, 6, 8, 32, 128), BF16),
            vmem((2, 2, 8, 32, 128), BF16),
            vmem((2, 16, 32, 128), BF16),
            vmem((2, 16, 32, 128), BF16),
            vmem((2, 16, 32, 128), BF16),
            vmem((2, 7, 2, 32, 128), BF16),
            vmem((4, 32, 128), F32),
            sem, sem, sem((NCHUNK,)),
            sem((NCHUNK,)), sem((NCHUNK,)), sem((NCHUNK,)),
            sem((NCHUNK,)), sem((NCHUNK,)), sem((NCHUNK,)),
            sem((8,)), sem((8,)), sem((2, 6)), sem((2, 6)), sem((2, 7)), sem((2, 7)), sem((3,)), sem((3,)),
        ],
        compiler_params=pltpu.CompilerParams(
            collective_id=0, has_side_effects=True, vmem_limit_bytes=58 * 1024 * 1024),
    )(cols, rows, live, row_lanes, integrals, orbitals)


def shards(integrals, slot_row_block, slot_column_block, shard_live_slots, orbitals):
    return applied(slot_column_block, slot_row_block, shard_live_slots, slot_row_block.reshape(1, SLOTS),
                   integrals.reshape(SLOTS * SIDE, 512), orbitals)


def solution(mesh):
    placed = (P("aux", None, None), P("aux"), P("aux"), P("aux"), P("occ", None))
    return jax.shard_map(
        shards, mesh=mesh, in_specs=placed, out_specs=P(None, ("aux", "occ")), check_vma=False
    )
```

```python
import jax
import jax.numpy as jnp
from jax import lax
from jax.experimental import pallas as pl
from jax.experimental.pallas import tpu as pltpu
from jax.sharding import PartitionSpec as P

MESH = pl.DeviceIdType.MESH
SLOTS = 128
SIDE = 64
NCHUNK = 8
CSLOTS = SLOTS // NCHUNK
CL = CSLOTS * SIDE
CT = CSLOTS * 128
TILES = 4
F32 = jnp.float32
BF16 = jnp.bfloat16


def swap_halves(v):
    return pltpu.roll(v, SIDE, v.ndim - 1)


def low_lanes(shape):
    return lax.broadcasted_iota(jnp.int32, shape, len(shape) - 1) < SIDE


def lanes_at(k, size):
    return pl.ds(pl.multiple_of(k * size, size), size)


def kernel(cols, rows, live, row_lanes, integrals, orbitals, out,
           orb, table, lists, maps, ints, gath, rr, hbuf, facc,
           e2, own, cbuf, crecv, ysend, yfar, yleft, yright, zsend, zrecv, xsend,
           orb_sem, map_sem, int_sem, send_l, send_r, send_f, recv_l, recv_r, recv_f,
           csend_sem, crecv_sem, ysend_sem, yrecv_sem, zsend_sem, zrecv_sem, xsend_sem, xrecv_sem):
    aux, me = lax.axis_index("aux"), lax.axis_index("occ")
    right, left = lax.rem(me + 1, 4), lax.rem(me + 3, 4)
    core = lax.rem(aux, 2)
    z = lax.rem(aux // 2, 8)
    y = aux // 16

    def at(yy, zz, cc):
        return ((yy * 8 + zz) * 2 + cc, me)

    other_core = at(y, z, 1 - core)
    up, down, far = lax.rem(y + 1, 4), lax.rem(y + 3, 4), lax.rem(y + 2, 4)
    dev_up, dev_down = at(up, z, core), at(down, z, core)

    orb_copy = pltpu.make_async_copy(orbitals, orb, orb_sem)
    orb_copy.start()

    def int_copy(c):
        here = pl.ds(c * CL, CL)
        return pltpu.make_async_copy(integrals.at[here], ints.at[here], int_sem.at[c])

    barrier = pltpu.get_barrier_semaphore()
    peers = [other_core, dev_up, dev_down]
    peers += [at(y, lax.rem(z + d, 8), core) for d in range(1, 8)]
    peers += [(aux, lax.rem(me + d, 4)) for d in range(1, 4)]
    for peer in peers:
        pl.semaphore_signal(barrier, inc=1, device_id=peer, device_id_type=MESH)

    across = jnp.broadcast_to(row_lanes[...], (SLOTS, 128))
    along = jnp.transpose(across)
    slot = lax.broadcasted_iota(jnp.int32, (SLOTS, 128), 0)
    lane = lax.broadcasted_iota(jnp.int32, (SLOTS, 128), 1)

    def last_of(hit):
        v = jnp.max(jnp.where(hit, slot, -1), axis=0, keepdims=True)
        return jnp.where(v < 0, SLOTS, v)

    for r in range(4):
        lists[r:r + 1, :] = last_of(along == lane + r * 128)
    lists[4:5, :] = last_of((along == across) & (slot < lane))
    lists[5:8, :] = jnp.full((3, 128), SLOTS, jnp.int32)
    map_copy = pltpu.make_async_copy(lists, maps, map_sem)
    map_copy.start()

    orb_copy.wait()
    for c in range(NCHUNK):
        int_copy(c).start()

    table[256] = jnp.zeros((32, 128), BF16)

    @pl.loop(0, 256, unroll=32)
    def _(k):
        table[k] = orb[:, lanes_at(k, 128)]

    def group(c, g):
        return gath.at[c, pl.ds(g * 32, 32)]

    def send(c, g_from, g_to, to, ssem, rsem):
        return pltpu.make_async_remote_copy(
            src_ref=group(c, g_from), dst_ref=group(c, g_to), send_sem=ssem.at[c], recv_sem=rsem.at[c],
            device_id=(aux, to), device_id_type=MESH)

    def to_left(c):
        return send(c, 0, 2, left, send_l, recv_r)

    def to_right(c):
        return send(c, 0, 1, right, send_r, recv_l)

    def onward(c):
        if c % 2 == 0:
            return send(c, 1, 3, right, send_f, recv_f)
        return send(c, 2, 3, left, send_f, recv_f)

    count = live[0]

    def column(s, half):
        b = cols[s]
        alive = jnp.minimum(jnp.maximum(count - s, 0), 1)
        return pltpu.roll(table[256 + ((b >> 1) - 256) * alive], ((b ^ half) & 1) * SIDE, 1)

    for c in range(NCHUNK):
        found = [column(c * CSLOTS + k, k % 2) for k in range(CSLOTS)]
        low = low_lanes((32, 128))
        for k in range(CSLOTS // 2):
            gath[c, 0:32, k * 128:(k + 1) * 128] = jnp.where(low, found[2 * k], found[2 * k + 1])
        if c == 0:
            pl.semaphore_wait(barrier, 13)
        to_left(c).start()
        to_right(c).start()

    for c in range(NCHUNK):
        blocks = [rows[c * CSLOTS + k] for k in range(CSLOTS)]
        tiles = [table[b >> 1] for b in blocks]
        low = low_lanes((32, 128))
        zero = jnp.zeros((32, 128), BF16)
        in_low = [jnp.where(low, pltpu.roll(t, (b & 1) * SIDE, 1), zero) for b, t in zip(blocks, tiles)]
        in_high = [jnp.where(low, zero, pltpu.roll(t, ((b & 1) ^ 1) * SIDE, 1)) for b, t in zip(blocks, tiles)]
        for k in range(CSLOTS):
            rr[c, 0:32, k * 128:(k + 1) * 128] = in_low[k]
            rr[c, 32:64, k * 128:(k + 1) * 128] = in_high[k]

    facc[...] = jnp.zeros_like(facc)

    def half(c, first, count):
        @pl.loop(0, CSLOTS // 2, unroll=8)
        def _(k):
            g = gath[c, first:first + count, lanes_at(k, 128)]
            low = low_lanes(g.shape)
            zero = jnp.zeros_like(g)
            lhs = jnp.concatenate([jnp.where(low, g, zero), jnp.where(low, zero, g)], 0)
            w = ints[lanes_at(c * (CSLOTS // 2) + k, 128), :]
            h = jnp.dot(lhs, w, preferred_element_type=F32).astype(BF16)
            for t in range(TILES):
                for n in range(2):
                    hbuf[c, t * 128 + first:t * 128 + first + count, lanes_at(2 * k + n, 128)] = (
                        h[n * count:(n + 1) * count, t * 128:(t + 1) * 128])

    for c in range(NCHUNK):
        to_left(c).wait_recv()
        to_right(c).wait_recv()
        onward(c).start()
        int_copy(c).wait()
        half(c, 0, 96)
    for c in range(NCHUNK):
        onward(c).wait_recv()
        half(c, 96, 32)
        facc[...] += lax.dot_general(rr[c], hbuf[c], (((1,), (1,)), ((), ())), preferred_element_type=F32)

    fit = facc[...].astype(BF16)
    map_copy.wait()
    e2[SLOTS] = jnp.zeros((32, 128), F32)
    for c in range(NCHUNK):
        @pl.loop(0, CSLOTS // 4, unroll=4)
        def _(k, c=c):
            v = jnp.dot(fit, hbuf[c, :, lanes_at(k, 512)], preferred_element_type=F32)
            low = low_lanes((32, 128))
            for n in range(4):
                s = c * CSLOTS + 4 * k + n
                here = slice(n * 128, (n + 1) * 128)
                u = jnp.where(low, v[:32, here], v[32:, here])
                e2[s] = u + swap_halves(u) + e2[maps[4, s]]

    order = [far, up, down, y]

    def dense(n, h, first, cc):
        low = low_lanes((32, 128))
        spots = [2 * ((first + m) // 2 * 8 + cc * 4 + 2 * h + m % 2) for m in range(8)]
        pairs = [(e2[maps[order[n], at]], e2[maps[order[n], at + 1]]) for at in spots]
        return [jnp.where(low, a, b) for a, b in pairs]

    def core_copy(n, h):
        k = h * 4 + n
        return pltpu.make_async_remote_copy(
            src_ref=cbuf.at[k], dst_ref=crecv.at[k], send_sem=csend_sem.at[k], recv_sem=crecv_sem.at[k],
            device_id=other_core, device_id_type=MESH)

    def share(n, h):
        for first in (0, 8):
            for m, v in enumerate(dense(n, h, first, 1 - core)):
                cbuf[h * 4 + n, first + m] = v.astype(BF16)
        core_copy(n, h).start()

    def summed(n, h, first):
        return [v + crecv[h * 4 + n, first + m].astype(F32) for m, v in enumerate(dense(n, h, first, core))]

    def y_copy(h, k, dst, dev):
        return pltpu.make_async_remote_copy(
            src_ref=ysend.at[h, k], dst_ref=dst, send_sem=ysend_sem.at[h, k], recv_sem=yrecv_sem.at[h, k],
            device_id=dev, device_id_type=MESH)

    first, last = pl.ds(0, 8), pl.ds(8, 8)

    def y_copies(h):
        return (
            y_copy(h, 0, yfar.at[h, 0], dev_up),
            y_copy(h, 1, yfar.at[h, 1], dev_down),
            y_copy(h, 2, yleft.at[h, last], dev_up),
            y_copy(h, 3, yright.at[h, first], dev_down),
            y_copy(h, 4, yleft.at[h, first], dev_up),
            y_copy(h, 5, yright.at[h, last], dev_down),
        )

    def fill(h, k, values):
        for m, v in enumerate(values):
            ysend[h, k, m] = v.astype(BF16)
        y_copies(h)[k].start()

    def send_far(h):
        core_copy(0, h).wait_recv()
        fill(h, 0, summed(0, h, 0))
        fill(h, 1, summed(0, h, 8))

    def send_near(h):
        core_copy(1, h).wait_recv()
        fill(h, 2, summed(1, h, 8))
        core_copy(2, h).wait_recv()
        fill(h, 3, summed(2, h, 0))

    def send_merged(h):
        cp = y_copies(h)
        cp[0].wait_recv()
        fill(h, 4, [v + yfar[h, 0, m].astype(F32) for m, v in enumerate(summed(1, h, 0))])
        cp[1].wait_recv()
        fill(h, 5, [v + yfar[h, 1, m].astype(F32) for m, v in enumerate(summed(2, h, 8))])

    share(0, 0)
    share(1, 0)
    share(2, 0)
    share(0, 1)
    send_far(0)
    send_near(0)
    share(1, 1)
    share(2, 1)
    send_far(1)
    send_merged(0)
    send_near(1)
    share(3, 0)
    share(3, 1)
    send_merged(1)

    def z_copy(h, d):
        to = lax.rem(z + d, 8)
        return pltpu.make_async_remote_copy(
            src_ref=zsend.at[h, pl.ds(pl.multiple_of(to * 2, 2), 2)], dst_ref=zrecv.at[h, d - 1],
            send_sem=zsend_sem.at[h, d - 1], recv_sem=zrecv_sem.at[h, d - 1],
            device_id=at(y, to, core), device_id_type=MESH)

    for h in range(2):
        core_copy(3, h).wait_recv()
        for cp in y_copies(h)[2:]:
            cp.wait_recv()

        for base in (0, 8):
            for m, v in enumerate(summed(3, h, base), base):
                v = v + yleft[h, m].astype(F32) + yright[h, m].astype(F32)
                own[h, m] = v
                zsend[h, m] = v.astype(BF16)
        for d in (4, 3, 5, 2, 6, 1, 7):
            z_copy(h, d).start()
    for h in range(2):
        for d in range(1, 8):
            z_copy(h, d).wait_recv()
        for m in range(2):
            v = own[h, z * 2 + m]
            for d in range(7):
                v = v + zrecv[h, d, m].astype(F32)
            xsend[2 * h + m] = v

    here = lanes_at(me, 32)
    out[here, :] = xsend[me]

    def x_copy(d):
        to = lax.rem(me + d, 4)
        return pltpu.make_async_remote_copy(
            src_ref=xsend.at[to], dst_ref=out.at[here],
            send_sem=xsend_sem.at[d - 1], recv_sem=xrecv_sem.at[d - 1],
            device_id=(aux, to), device_id_type=MESH)

    for d in (2, 1, 3):
        x_copy(d).start()
    for c in range(NCHUNK):
        to_left(c).wait_send()
        to_right(c).wait_send()
        onward(c).wait_send()
    for h in range(2):
        for n in range(4):
            core_copy(n, h).wait_send()
        for cp in y_copies(h):
            cp.wait_send()
        for d in range(1, 8):
            z_copy(h, d).wait_send()
    for d in range(1, 4):
        x_copy(d).wait()


def applied(cols, rows, live, row_lanes, integrals, orbitals):
    sem = pltpu.SemaphoreType.DMA
    vmem = pltpu.VMEM
    return pl.pallas_call(
        kernel,
        out_shape=jax.ShapeDtypeStruct((128, 128), F32),
        in_specs=[pl.BlockSpec(memory_space=pltpu.SMEM)] * 3 + [pl.BlockSpec(memory_space=pltpu.VMEM)]
        + [pl.BlockSpec(memory_space=pl.ANY)] * 2,
        out_specs=pl.BlockSpec(memory_space=pltpu.VMEM),
        scratch_shapes=[
            vmem((32, 32768), BF16),
            vmem((257, 32, 128), BF16),
            vmem((8, 128), jnp.int32),
            pltpu.SMEM((8, 128), jnp.int32),
            vmem((SLOTS * SIDE, 512), BF16),
            vmem((NCHUNK, 128, CL), BF16),
            vmem((NCHUNK, 64, CT), BF16),
            vmem((NCHUNK, 512, CT), BF16),
            vmem((64, 512), F32),
            vmem((SLOTS + 1, 32, 128), F32),
            vmem((2, 16, 32, 128), F32),
            vmem((8, 16, 32, 128), BF16),
            vmem((8, 16, 32, 128), BF16),
            vmem((2, 6, 8, 32, 128), BF16),
            vmem((2, 2, 8, 32, 128), BF16),
            vmem((2, 16, 32, 128), BF16),
            vmem((2, 16, 32, 128), BF16),
            vmem((2, 16, 32, 128), BF16),
            vmem((2, 7, 2, 32, 128), BF16),
            vmem((4, 32, 128), F32),
            sem, sem, sem((NCHUNK,)),
            sem((NCHUNK,)), sem((NCHUNK,)), sem((NCHUNK,)),
            sem((NCHUNK,)), sem((NCHUNK,)), sem((NCHUNK,)),
            sem((8,)), sem((8,)), sem((2, 6)), sem((2, 6)), sem((2, 7)), sem((2, 7)), sem((3,)), sem((3,)),
        ],
        compiler_params=pltpu.CompilerParams(
            collective_id=0, has_side_effects=True, vmem_limit_bytes=58 * 1024 * 1024),
    )(cols, rows, live, row_lanes, integrals, orbitals)


def shards(integrals, slot_row_block, slot_column_block, shard_live_slots, orbitals):
    return applied(slot_column_block, slot_row_block, shard_live_slots, slot_row_block.reshape(1, SLOTS),
                   integrals.reshape(SLOTS * SIDE, 512), orbitals)


def solution(mesh):
    placed = (P("aux", None, None), P("aux"), P("aux"), P("aux"), P("occ", None))
    return jax.shard_map(
        shards, mesh=mesh, in_specs=placed, out_specs=P(None, ("aux", "occ")), check_vma=False
    )
```

```python
import jax
import jax.numpy as jnp
from jax import lax
from jax.experimental import pallas as pl
from jax.experimental.pallas import tpu as pltpu
from jax.sharding import PartitionSpec as P

MESH = pl.DeviceIdType.MESH
SLOTS = 128
SIDE = 64
NCHUNK = 8
CSLOTS = SLOTS // NCHUNK
CL = CSLOTS * SIDE
CT = CSLOTS * 128
TILES = 4
F32 = jnp.float32
BF16 = jnp.bfloat16


def swap_halves(v):
    return pltpu.roll(v, SIDE, v.ndim - 1)


def low_lanes(shape):
    return lax.broadcasted_iota(jnp.int32, shape, len(shape) - 1) < SIDE


def lanes_at(k, size):
    return pl.ds(pl.multiple_of(k * size, size), size)


def kernel(cols, rows, live, row_lanes, integrals, orbitals, out,
           orb, table, lists, maps, ints, gath, rr, hbuf, facc,
           e2, own, cbuf, crecv, ysend, yfar, yleft, yright, zsend, zrecv, xsend,
           orb_sem, map_sem, int_sem, send_l, send_r, send_f, recv_l, recv_r, recv_f,
           csend_sem, crecv_sem, ysend_sem, yrecv_sem, zsend_sem, zrecv_sem, xsend_sem, xrecv_sem):
    aux, me = lax.axis_index("aux"), lax.axis_index("occ")
    right, left = lax.rem(me + 1, 4), lax.rem(me + 3, 4)
    core = lax.rem(aux, 2)
    z = lax.rem(aux // 2, 8)
    y = aux // 16

    def at(yy, zz, cc):
        return ((yy * 8 + zz) * 2 + cc, me)

    other_core = at(y, z, 1 - core)
    up, down, far = lax.rem(y + 1, 4), lax.rem(y + 3, 4), lax.rem(y + 2, 4)
    dev_up, dev_down = at(up, z, core), at(down, z, core)

    orb_copy = pltpu.make_async_copy(orbitals, orb, orb_sem)
    orb_copy.start()

    def int_copy(c):
        here = pl.ds(c * CL, CL)
        return pltpu.make_async_copy(integrals.at[here], ints.at[here], int_sem.at[c])

    barrier = pltpu.get_barrier_semaphore()
    peers = [other_core, dev_up, dev_down]
    peers += [at(y, lax.rem(z + d, 8), core) for d in range(1, 8)]
    peers += [(aux, lax.rem(me + d, 4)) for d in range(1, 4)]
    for peer in peers:
        pl.semaphore_signal(barrier, inc=1, device_id=peer, device_id_type=MESH)

    across = jnp.broadcast_to(row_lanes[...], (SLOTS, 128))
    along = jnp.transpose(across)
    slot = lax.broadcasted_iota(jnp.int32, (SLOTS, 128), 0)
    lane = lax.broadcasted_iota(jnp.int32, (SLOTS, 128), 1)

    def last_of(hit):
        v = jnp.max(jnp.where(hit, slot, -1), axis=0, keepdims=True)
        return jnp.where(v < 0, SLOTS, v)

    for r in range(4):
        lists[r:r + 1, :] = last_of(along == lane + r * 128)
    lists[4:5, :] = last_of((along == across) & (slot < lane))
    lists[5:8, :] = jnp.full((3, 128), SLOTS, jnp.int32)
    map_copy = pltpu.make_async_copy(lists, maps, map_sem)
    map_copy.start()

    orb_copy.wait()
    for c in range(NCHUNK):
        int_copy(c).start()

    table[256] = jnp.zeros((32, 128), BF16)

    @pl.loop(0, 256, unroll=32)
    def _(k):
        table[k] = orb[:, lanes_at(k, 128)]

    def group(c, g):
        return gath.at[c, pl.ds(g * 32, 32)]

    def send(c, g_from, g_to, to, ssem, rsem):
        return pltpu.make_async_remote_copy(
            src_ref=group(c, g_from), dst_ref=group(c, g_to), send_sem=ssem.at[c], recv_sem=rsem.at[c],
            device_id=(aux, to), device_id_type=MESH)

    def to_left(c):
        return send(c, 0, 2, left, send_l, recv_r)

    def to_right(c):
        return send(c, 0, 1, right, send_r, recv_l)

    def onward(c):
        if c % 2 == 0:
            return send(c, 1, 3, right, send_f, recv_f)
        return send(c, 2, 3, left, send_f, recv_f)

    count = live[0]

    def column(s, half):
        b = cols[s]
        alive = jnp.minimum(jnp.maximum(count - s, 0), 1)
        return pltpu.roll(table[256 + ((b >> 1) - 256) * alive], ((b ^ half) & 1) * SIDE, 1)

    for c in range(NCHUNK):
        found = [column(c * CSLOTS + k, k % 2) for k in range(CSLOTS)]
        low = low_lanes((32, 128))
        for k in range(CSLOTS // 2):
            gath[c, 0:32, k * 128:(k + 1) * 128] = jnp.where(low, found[2 * k], found[2 * k + 1])
        if c == 0:
            pl.semaphore_wait(barrier, 13)
        to_left(c).start()
        to_right(c).start()

    for c in range(NCHUNK):
        blocks = [rows[c * CSLOTS + k] for k in range(CSLOTS)]
        tiles = [table[b >> 1] for b in blocks]
        low = low_lanes((32, 128))
        zero = jnp.zeros((32, 128), BF16)
        in_low = [jnp.where(low, pltpu.roll(t, (b & 1) * SIDE, 1), zero) for b, t in zip(blocks, tiles)]
        in_high = [jnp.where(low, zero, pltpu.roll(t, ((b & 1) ^ 1) * SIDE, 1)) for b, t in zip(blocks, tiles)]
        for k in range(CSLOTS):
            rr[c, 0:32, k * 128:(k + 1) * 128] = in_low[k]
            rr[c, 32:64, k * 128:(k + 1) * 128] = in_high[k]

    facc[...] = jnp.zeros_like(facc)

    def half(c, first, count):
        base = 4 * first

        @pl.loop(0, CSLOTS // 2, unroll=8)
        def _(k):
            g = gath[c, first:first + count, lanes_at(k, 128)]
            low = low_lanes(g.shape)
            zero = jnp.zeros_like(g)
            lhs = jnp.concatenate([jnp.where(low, g, zero), jnp.where(low, zero, g)], 0)
            w = ints[lanes_at(c * (CSLOTS // 2) + k, 128), :]
            h = jnp.dot(lhs, w, preferred_element_type=F32).astype(BF16)
            for t in range(TILES):
                for n in range(2):
                    hbuf[c, base + t * count:base + (t + 1) * count, lanes_at(2 * k + n, 128)] = (
                        h[n * count:(n + 1) * count, t * 128:(t + 1) * 128])
        rows_here = slice(base, base + 4 * count)
        facc[:, rows_here] += lax.dot_general(
            rr[c], hbuf[c, rows_here, :], (((1,), (1,)), ((), ())), preferred_element_type=F32)

    for c in range(NCHUNK):
        to_left(c).wait_recv()
        to_right(c).wait_recv()
        onward(c).start()
        int_copy(c).wait()
        half(c, 0, 96)
    for c in range(NCHUNK):
        onward(c).wait_recv()
        half(c, 96, 32)

    fit = facc[...].astype(BF16)
    map_copy.wait()
    e2[SLOTS] = jnp.zeros((32, 128), F32)
    for c in range(NCHUNK):
        @pl.loop(0, CSLOTS // 4, unroll=4)
        def _(k, c=c):
            v = jnp.dot(fit, hbuf[c, :, lanes_at(k, 512)], preferred_element_type=F32)
            low = low_lanes((32, 128))
            for n in range(4):
                s = c * CSLOTS + 4 * k + n
                here = slice(n * 128, (n + 1) * 128)
                u = jnp.where(low, v[:32, here], v[32:, here])
                e2[s] = u + swap_halves(u) + e2[maps[4, s]]

    order = [far, up, down, y]
    owner = [lax.rem(me + d, 4) for d in (2, 1, 3)] + [me]

    def dense(n, h, first, count, cc):
        low = low_lanes((32, 128))
        spots = [2 * ((first + m) * 8 + cc * 4 + owner[h]) for m in range(count)]
        pairs = [(e2[maps[order[n], spot]], e2[maps[order[n], spot + 1]]) for spot in spots]
        return [jnp.where(low, a, b) for a, b in pairs]

    def core_copy(n, h):
        k = h * 4 + n
        return pltpu.make_async_remote_copy(
            src_ref=cbuf.at[k], dst_ref=crecv.at[k], send_sem=csend_sem.at[k], recv_sem=crecv_sem.at[k],
            device_id=other_core, device_id_type=MESH)

    def share(n, h):
        for m, v in enumerate(dense(n, h, 0, 8, 1 - core)):
            cbuf[h * 4 + n, m] = v.astype(BF16)
        core_copy(n, h).start()

    def summed(n, h, first, count):
        found = dense(n, h, first, count, core)
        return [v + crecv[h * 4 + n, first + m].astype(F32) for m, v in enumerate(found)]

    def y_copy(h, k):
        near, away = pl.ds(0, 4), pl.ds(4, 4)
        dst = (yfar.at[h, 0], yfar.at[h, 1], yleft.at[h, away], yright.at[h, near],
               yleft.at[h, near], yright.at[h, away])[k]
        return pltpu.make_async_remote_copy(
            src_ref=ysend.at[h, k], dst_ref=dst, send_sem=ysend_sem.at[h, k], recv_sem=yrecv_sem.at[h, k],
            device_id=dev_down if k % 2 else dev_up, device_id_type=MESH)

    def fill(h, k, values):
        for m, v in enumerate(values):
            ysend[h, k, m] = v.astype(BF16)
        y_copy(h, k).start()

    def send_direct(h):
        core_copy(0, h).wait_recv()
        fill(h, 0, summed(0, h, 0, 4))
        fill(h, 1, summed(0, h, 4, 4))
        core_copy(1, h).wait_recv()
        fill(h, 2, summed(1, h, 4, 4))
        core_copy(2, h).wait_recv()
        fill(h, 3, summed(2, h, 0, 4))

    def send_merged(h):
        y_copy(h, 0).wait_recv()
        fill(h, 4, [v + yfar[h, 0, m].astype(F32) for m, v in enumerate(summed(1, h, 0, 4))])
        y_copy(h, 1).wait_recv()
        fill(h, 5, [v + yfar[h, 1, m].astype(F32) for m, v in enumerate(summed(2, h, 4, 4))])

    def z_copy(h, d):
        to = lax.rem(z + d, 8)
        return pltpu.make_async_remote_copy(
            src_ref=zsend.at[h, to], dst_ref=zrecv.at[h, d - 1],
            send_sem=zsend_sem.at[h, d - 1], recv_sem=zrecv_sem.at[h, d - 1],
            device_id=at(y, to, core), device_id_type=MESH)

    def send_z(h):
        core_copy(3, h).wait_recv()
        for k in range(2, 6):
            y_copy(h, k).wait_recv()
        for m, v in enumerate(summed(3, h, 0, 8)):
            v = v + yleft[h, m].astype(F32) + yright[h, m].astype(F32)
            own[h, m] = v
            zsend[h, m] = v.astype(BF16)
        for d in (4, 3, 5, 2, 6, 1, 7):
            z_copy(h, d).start()

    here = lanes_at(me, 32)

    def x_copy(h):
        return pltpu.make_async_remote_copy(
            src_ref=xsend.at[h], dst_ref=out.at[here], send_sem=xsend_sem.at[h], recv_sem=xrecv_sem.at[h],
            device_id=(aux, owner[h]), device_id_type=MESH)

    def finish(h):
        for d in range(1, 8):
            z_copy(h, d).wait_recv()
        v = own[h, z]
        for d in range(7):
            v = v + zrecv[h, d].astype(F32)
        if h < 3:
            xsend[h] = v
            x_copy(h).start()
        else:
            out[here, :] = v

    def shares(*parts):
        for n, h in parts:
            share(n, h)

    shares((0, 0), (1, 0), (2, 0), (0, 1))
    send_direct(0)
    shares((1, 1), (2, 1), (0, 2))
    send_direct(1)
    send_merged(0)
    shares((1, 2), (2, 2), (0, 3))
    send_direct(2)
    send_merged(1)
    shares((1, 3), (2, 3), (3, 0), (3, 1))
    send_direct(3)
    send_z(0)
    send_merged(2)
    shares((3, 2), (3, 3))
    send_z(1)
    send_merged(3)
    finish(0)
    send_z(2)
    finish(1)
    send_z(3)
    finish(2)
    finish(3)

    for c in range(NCHUNK):
        to_left(c).wait_send()
        to_right(c).wait_send()
        onward(c).wait_send()
    for h in range(4):
        for n in range(4):
            core_copy(n, h).wait_send()
        for k in range(6):
            y_copy(h, k).wait_send()
        for d in range(1, 8):
            z_copy(h, d).wait_send()
        if h < 3:
            x_copy(h).wait()


def applied(cols, rows, live, row_lanes, integrals, orbitals):
    sem = pltpu.SemaphoreType.DMA
    vmem = pltpu.VMEM
    return pl.pallas_call(
        kernel,
        out_shape=jax.ShapeDtypeStruct((128, 128), F32),
        in_specs=[pl.BlockSpec(memory_space=pltpu.SMEM)] * 3 + [pl.BlockSpec(memory_space=pltpu.VMEM)]
        + [pl.BlockSpec(memory_space=pl.ANY)] * 2,
        out_specs=pl.BlockSpec(memory_space=pltpu.VMEM),
        scratch_shapes=[
            vmem((32, 32768), BF16),
            vmem((257, 32, 128), BF16),
            vmem((8, 128), jnp.int32),
            pltpu.SMEM((8, 128), jnp.int32),
            vmem((SLOTS * SIDE, 512), BF16),
            vmem((NCHUNK, 128, CL), BF16),
            vmem((NCHUNK, 64, CT), BF16),
            vmem((NCHUNK, 512, CT), BF16),
            vmem((64, 512), F32),
            vmem((SLOTS + 1, 32, 128), F32),
            vmem((4, 8, 32, 128), F32),
            vmem((16, 8, 32, 128), BF16),
            vmem((16, 8, 32, 128), BF16),
            vmem((4, 6, 4, 32, 128), BF16),
            vmem((4, 2, 4, 32, 128), BF16),
            vmem((4, 8, 32, 128), BF16),
            vmem((4, 8, 32, 128), BF16),
            vmem((4, 8, 32, 128), BF16),
            vmem((4, 7, 32, 128), BF16),
            vmem((3, 32, 128), F32),
            sem, sem, sem((NCHUNK,)),
            sem((NCHUNK,)), sem((NCHUNK,)), sem((NCHUNK,)),
            sem((NCHUNK,)), sem((NCHUNK,)), sem((NCHUNK,)),
            sem((16,)), sem((16,)), sem((4, 6)), sem((4, 6)), sem((4, 7)), sem((4, 7)), sem((3,)), sem((3,)),
        ],
        compiler_params=pltpu.CompilerParams(
            collective_id=0, has_side_effects=True, vmem_limit_bytes=58 * 1024 * 1024),
    )(cols, rows, live, row_lanes, integrals, orbitals)


def shards(integrals, slot_row_block, slot_column_block, shard_live_slots, orbitals):
    return applied(slot_column_block, slot_row_block, shard_live_slots, slot_row_block.reshape(1, SLOTS),
                   integrals.reshape(SLOTS * SIDE, 512), orbitals)


def solution(mesh):
    placed = (P("aux", None, None), P("aux"), P("aux"), P("aux"), P("occ", None))
    return jax.shard_map(
        shards, mesh=mesh, in_specs=placed, out_specs=P(None, ("aux", "occ")), check_vma=False
    )
```

```python
import jax
import jax.numpy as jnp
from jax import lax
from jax.experimental import pallas as pl
from jax.experimental.pallas import tpu as pltpu
from jax.sharding import PartitionSpec as P

MESH = pl.DeviceIdType.MESH
SLOTS = 128
SIDE = 64
NCHUNK = 8
CSLOTS = SLOTS // NCHUNK
CL = CSLOTS * SIDE
CT = CSLOTS * 128
TILES = 4
F32 = jnp.float32
BF16 = jnp.bfloat16


def swap_halves(v):
    return pltpu.roll(v, SIDE, v.ndim - 1)


def low_lanes(shape):
    return lax.broadcasted_iota(jnp.int32, shape, len(shape) - 1) < SIDE


def lanes_at(k, size):
    return pl.ds(pl.multiple_of(k * size, size), size)


def kernel(cols, rows, live, row_lanes, integrals, orbitals, out,
           orb, table, lists, maps, ints, gath, rr, hbuf, facc,
           e2, own, cbuf, crecv, ysend, yfar, yleft, yright, zsend, zrecv, xsend,
           orb_sem, map_sem, int_sem, send_l, send_r, send_f, recv_l, recv_r, recv_f,
           csend_sem, crecv_sem, ysend_sem, yrecv_sem, zsend_sem, zrecv_sem, xsend_sem, xrecv_sem):
    aux, me = lax.axis_index("aux"), lax.axis_index("occ")
    right, left = lax.rem(me + 1, 4), lax.rem(me + 3, 4)
    core = lax.rem(aux, 2)
    z = lax.rem(aux // 2, 8)
    y = aux // 16

    def at(yy, zz, cc):
        return ((yy * 8 + zz) * 2 + cc, me)

    other_core = at(y, z, 1 - core)
    up, down, far = lax.rem(y + 1, 4), lax.rem(y + 3, 4), lax.rem(y + 2, 4)
    dev_up, dev_down = at(up, z, core), at(down, z, core)

    orb_copy = pltpu.make_async_copy(orbitals, orb, orb_sem)
    orb_copy.start()

    def int_copy(c):
        here = pl.ds(c * CL, CL)
        return pltpu.make_async_copy(integrals.at[here], ints.at[here], int_sem.at[c])

    barrier = pltpu.get_barrier_semaphore()
    peers = [other_core, dev_up, dev_down]
    peers += [at(y, lax.rem(z + d, 8), core) for d in range(1, 8)]
    peers += [(aux, lax.rem(me + d, 4)) for d in range(1, 4)]
    for peer in peers:
        pl.semaphore_signal(barrier, inc=1, device_id=peer, device_id_type=MESH)

    across = jnp.broadcast_to(row_lanes[...], (SLOTS, 128))
    along = jnp.transpose(across)
    slot = lax.broadcasted_iota(jnp.int32, (SLOTS, 128), 0)
    lane = lax.broadcasted_iota(jnp.int32, (SLOTS, 128), 1)

    def last_of(hit):
        v = jnp.max(jnp.where(hit, slot, -1), axis=0, keepdims=True)
        return jnp.where(v < 0, SLOTS, v)

    for r in range(4):
        lists[r:r + 1, :] = last_of(along == lane + r * 128)
    lists[4:5, :] = last_of((along == across) & (slot < lane))
    lists[5:8, :] = jnp.full((3, 128), SLOTS, jnp.int32)
    map_copy = pltpu.make_async_copy(lists, maps, map_sem)
    map_copy.start()

    orb_copy.wait()
    for c in range(NCHUNK):
        int_copy(c).start()

    table[256] = jnp.zeros((32, 128), BF16)

    @pl.loop(0, 256, unroll=32)
    def _(k):
        table[k] = orb[:, lanes_at(k, 128)]

    def group(c, g):
        return gath.at[c, pl.ds(g * 32, 32)]

    def send(c, g_from, g_to, to, ssem, rsem):
        return pltpu.make_async_remote_copy(
            src_ref=group(c, g_from), dst_ref=group(c, g_to), send_sem=ssem.at[c], recv_sem=rsem.at[c],
            device_id=(aux, to), device_id_type=MESH)

    def to_left(c):
        return send(c, 0, 2, left, send_l, recv_r)

    def to_right(c):
        return send(c, 0, 1, right, send_r, recv_l)

    def onward(c):
        if c % 2 == 0:
            return send(c, 1, 3, right, send_f, recv_f)
        return send(c, 2, 3, left, send_f, recv_f)

    count = live[0]

    def column(s, half):
        b = cols[s]
        alive = jnp.minimum(jnp.maximum(count - s, 0), 1)
        return pltpu.roll(table[256 + ((b >> 1) - 256) * alive], ((b ^ half) & 1) * SIDE, 1)

    for c in range(NCHUNK):
        found = [column(c * CSLOTS + k, k % 2) for k in range(CSLOTS)]
        low = low_lanes((32, 128))
        for k in range(CSLOTS // 2):
            gath[c, 0:32, k * 128:(k + 1) * 128] = jnp.where(low, found[2 * k], found[2 * k + 1])
        if c == 0:
            pl.semaphore_wait(barrier, 13)
        to_left(c).start()
        to_right(c).start()

    for c in range(NCHUNK):
        blocks = [rows[c * CSLOTS + k] for k in range(CSLOTS)]
        tiles = [table[b >> 1] for b in blocks]
        low = low_lanes((32, 128))
        zero = jnp.zeros((32, 128), BF16)
        in_low = [jnp.where(low, pltpu.roll(t, (b & 1) * SIDE, 1), zero) for b, t in zip(blocks, tiles)]
        in_high = [jnp.where(low, zero, pltpu.roll(t, ((b & 1) ^ 1) * SIDE, 1)) for b, t in zip(blocks, tiles)]
        for k in range(CSLOTS):
            rr[c, 0:32, k * 128:(k + 1) * 128] = in_low[k]
            rr[c, 32:64, k * 128:(k + 1) * 128] = in_high[k]

    facc[...] = jnp.zeros_like(facc)

    def half(c, first, count):
        base = 4 * first

        @pl.loop(0, CSLOTS // 2, unroll=8)
        def _(k):
            g = gath[c, first:first + count, lanes_at(k, 128)]
            low = low_lanes(g.shape)
            zero = jnp.zeros_like(g)
            lhs = jnp.concatenate([jnp.where(low, g, zero), jnp.where(low, zero, g)], 0)
            w = ints[lanes_at(c * (CSLOTS // 2) + k, 128), :]
            h = jnp.dot(lhs, w, preferred_element_type=F32).astype(BF16)
            for t in range(TILES):
                for n in range(2):
                    hbuf[c, base + t * count:base + (t + 1) * count, lanes_at(2 * k + n, 128)] = (
                        h[n * count:(n + 1) * count, t * 128:(t + 1) * 128])
        rows_here = slice(base, base + 4 * count)
        facc[:, rows_here] += lax.dot_general(
            rr[c], hbuf[c, rows_here, :], (((1,), (1,)), ((), ())), preferred_element_type=F32)

    for c in range(NCHUNK):
        to_left(c).wait_recv()
        to_right(c).wait_recv()
        onward(c).start()
        int_copy(c).wait()
        half(c, 0, 96)
    for c in range(NCHUNK):
        onward(c).wait_recv()
        half(c, 96, 32)

    fit = facc[...].astype(BF16)
    map_copy.wait()
    e2[SLOTS] = jnp.zeros((32, 128), F32)
    for c in range(NCHUNK):
        @pl.loop(0, CSLOTS // 4, unroll=4)
        def _(k, c=c):
            v = jnp.dot(fit, hbuf[c, :, lanes_at(k, 512)], preferred_element_type=F32)
            low = low_lanes((32, 128))
            for n in range(4):
                s = c * CSLOTS + 4 * k + n
                here = slice(n * 128, (n + 1) * 128)
                u = jnp.where(low, v[:32, here], v[32:, here])
                e2[s] = u + swap_halves(u) + e2[maps[4, s]]

    order = [far, up, down, y]
    owner = [lax.rem(me + d, 4) for d in (2, 1, 3)] + [me]

    def dense(n, h, first, count, cc):
        low = low_lanes((32, 128))
        spots = [2 * ((first + m) * 8 + cc * 4 + owner[h]) for m in range(count)]
        pairs = [(e2[maps[order[n], spot]], e2[maps[order[n], spot + 1]]) for spot in spots]
        return [jnp.where(low, a, b) for a, b in pairs]

    def core_copy(n, h):
        k = h * 4 + n
        return pltpu.make_async_remote_copy(
            src_ref=cbuf.at[k], dst_ref=crecv.at[k], send_sem=csend_sem.at[k], recv_sem=crecv_sem.at[k],
            device_id=other_core, device_id_type=MESH)

    def share(n, h):
        for m, v in enumerate(dense(n, h, 0, 8, 1 - core)):
            cbuf[h * 4 + n, m] = v.astype(BF16)
        core_copy(n, h).start()

    def summed(n, h, first, count):
        found = dense(n, h, first, count, core)
        return [v + crecv[h * 4 + n, first + m].astype(F32) for m, v in enumerate(found)]

    def y_copy(h, k):
        near, away = pl.ds(0, 4), pl.ds(4, 4)
        dst = (yfar.at[h, 0], yfar.at[h, 1], yleft.at[h, away], yright.at[h, near],
               yleft.at[h, near], yright.at[h, away])[k]
        return pltpu.make_async_remote_copy(
            src_ref=ysend.at[h, k], dst_ref=dst, send_sem=ysend_sem.at[h, k], recv_sem=yrecv_sem.at[h, k],
            device_id=dev_down if k % 2 else dev_up, device_id_type=MESH)

    def fill(h, k, values):
        for m, v in enumerate(values):
            ysend[h, k, m] = v.astype(BF16)
        y_copy(h, k).start()

    def send_far(h):
        core_copy(0, h).wait_recv()
        fill(h, 0, summed(0, h, 0, 4))
        fill(h, 1, summed(0, h, 4, 4))

    def send_near(h):
        core_copy(1, h).wait_recv()
        fill(h, 2, summed(1, h, 4, 4))
        core_copy(2, h).wait_recv()
        fill(h, 3, summed(2, h, 0, 4))

    def send_merged(h):
        y_copy(h, 0).wait_recv()
        fill(h, 4, [v + yfar[h, 0, m].astype(F32) for m, v in enumerate(summed(1, h, 0, 4))])
        y_copy(h, 1).wait_recv()
        fill(h, 5, [v + yfar[h, 1, m].astype(F32) for m, v in enumerate(summed(2, h, 4, 4))])

    def z_copy(h, d):
        to = lax.rem(z + d, 8)
        return pltpu.make_async_remote_copy(
            src_ref=zsend.at[h, to], dst_ref=zrecv.at[h, d - 1],
            send_sem=zsend_sem.at[h, d - 1], recv_sem=zrecv_sem.at[h, d - 1],
            device_id=at(y, to, core), device_id_type=MESH)

    def send_z(h):
        core_copy(3, h).wait_recv()
        for k in range(2, 6):
            y_copy(h, k).wait_recv()
        for m, v in enumerate(summed(3, h, 0, 8)):
            v = v + yleft[h, m].astype(F32) + yright[h, m].astype(F32)
            own[h, m] = v
            zsend[h, m] = v.astype(BF16)
        for d in (4, 3, 5, 2, 6, 1, 7):
            z_copy(h, d).start()

    here = lanes_at(me, 32)

    def x_copy(h):
        return pltpu.make_async_remote_copy(
            src_ref=xsend.at[h], dst_ref=out.at[here], send_sem=xsend_sem.at[h], recv_sem=xrecv_sem.at[h],
            device_id=(aux, owner[h]), device_id_type=MESH)

    def finish(h):
        for d in range(1, 8):
            z_copy(h, d).wait_recv()
        v = own[h, z]
        for d in range(7):
            v = v + zrecv[h, d].astype(F32)
        if h < 3:
            xsend[h] = v
            x_copy(h).start()
        else:
            out[here, :] = v

    def shares(*parts):
        for n, h in parts:
            share(n, h)

    shares((0, 0), (1, 0), (2, 0), (0, 1), (0, 2))
    send_far(0)
    send_near(0)
    send_far(1)
    send_far(2)
    shares((0, 3), (1, 1), (2, 1))
    send_merged(0)
    send_far(3)
    shares((3, 0), (1, 2), (2, 2))
    send_near(1)
    send_merged(1)
    shares((3, 1), (1, 3), (2, 3))
    send_near(2)
    send_z(0)
    send_merged(2)
    shares((3, 2), (3, 3))
    send_near(3)
    send_merged(3)
    send_z(1)
    finish(0)
    send_z(2)
    finish(1)
    send_z(3)
    finish(2)
    finish(3)

    for c in range(NCHUNK):
        to_left(c).wait_send()
        to_right(c).wait_send()
        onward(c).wait_send()
    for h in range(4):
        for n in range(4):
            core_copy(n, h).wait_send()
        for k in range(6):
            y_copy(h, k).wait_send()
        for d in range(1, 8):
            z_copy(h, d).wait_send()
        if h < 3:
            x_copy(h).wait()


def applied(cols, rows, live, row_lanes, integrals, orbitals):
    sem = pltpu.SemaphoreType.DMA
    vmem = pltpu.VMEM
    return pl.pallas_call(
        kernel,
        out_shape=jax.ShapeDtypeStruct((128, 128), F32),
        in_specs=[pl.BlockSpec(memory_space=pltpu.SMEM)] * 3 + [pl.BlockSpec(memory_space=pltpu.VMEM)]
        + [pl.BlockSpec(memory_space=pl.ANY)] * 2,
        out_specs=pl.BlockSpec(memory_space=pltpu.VMEM),
        scratch_shapes=[
            vmem((32, 32768), BF16),
            vmem((257, 32, 128), BF16),
            vmem((8, 128), jnp.int32),
            pltpu.SMEM((8, 128), jnp.int32),
            vmem((SLOTS * SIDE, 512), BF16),
            vmem((NCHUNK, 128, CL), BF16),
            vmem((NCHUNK, 64, CT), BF16),
            vmem((NCHUNK, 512, CT), BF16),
            vmem((64, 512), F32),
            vmem((SLOTS + 1, 32, 128), F32),
            vmem((4, 8, 32, 128), F32),
            vmem((16, 8, 32, 128), BF16),
            vmem((16, 8, 32, 128), BF16),
            vmem((4, 6, 4, 32, 128), BF16),
            vmem((4, 2, 4, 32, 128), BF16),
            vmem((4, 8, 32, 128), BF16),
            vmem((4, 8, 32, 128), BF16),
            vmem((4, 8, 32, 128), BF16),
            vmem((4, 7, 32, 128), BF16),
            vmem((3, 32, 128), F32),
            sem, sem, sem((NCHUNK,)),
            sem((NCHUNK,)), sem((NCHUNK,)), sem((NCHUNK,)),
            sem((NCHUNK,)), sem((NCHUNK,)), sem((NCHUNK,)),
            sem((16,)), sem((16,)), sem((4, 6)), sem((4, 6)), sem((4, 7)), sem((4, 7)), sem((3,)), sem((3,)),
        ],
        compiler_params=pltpu.CompilerParams(
            collective_id=0, has_side_effects=True, vmem_limit_bytes=58 * 1024 * 1024),
    )(cols, rows, live, row_lanes, integrals, orbitals)


def shards(integrals, slot_row_block, slot_column_block, shard_live_slots, orbitals):
    return applied(slot_column_block, slot_row_block, shard_live_slots, slot_row_block.reshape(1, SLOTS),
                   integrals.reshape(SLOTS * SIDE, 512), orbitals)


def solution(mesh):
    placed = (P("aux", None, None), P("aux"), P("aux"), P("aux"), P("occ", None))
    return jax.shard_map(
        shards, mesh=mesh, in_specs=placed, out_specs=P(None, ("aux", "occ")), check_vma=False
    )
```
